32 devices in a mesh: groups: 2 (over x), tensor: 16 (over z, y, core).
Axes of the slice: x: 2, y: 2, z: 4, core: 2. Of those that a mesh axis runs over, the one named last changes fastest.
Arguments:
- tokens_in: bfloat16 [1024, 8192], P(('groups', 'tensor')), parts along dimension 0, may hold values from -4 to 4
- mask_pos: int32 [4, 64], P('groups'), parts along dimension 0, may hold values from 0 to 255
- step_index: int32 [4], P('groups'), parts along dimension 0, may hold values from 0 to 63
- mask_embed: bfloat16 [8192], replicated, may hold values from -5 to 5
- time_table: bfloat16 [64, 8192], replicated, may hold values from -4 to 4
- norm_gain: float32 [8192], replicated, may hold values from 0.5 to 1.5
- w_qkv: bfloat16 [3, 8192, 2048], P(None, None, 'tensor'), may hold values from -0.0625 to 0.0625
- qk_gain: float32 [2, 2048], P(None, 'tensor'), may hold values from 1 to 2
- w_out: bfloat16 [2048, 8192], P('tensor'), may hold values from -0.5 to 0.5
Outputs:
- mixed: bfloat16 [1024, 8192], P('groups', 'tensor'), parts along dimension 0
The draws below stay inside these ranges and needn't reach their ends.
There are 2 independent parts, one for each index of `groups`. The reference program is written for one: setup_inputs(seed, part) draws one part's arguments, and reference() takes and returns one part's arrays. A program takes and returns all parts, laid end to end along the dimension named above; an argument that names none is the same for every part. Nothing has to cross between parts.
Inputs may be any that keep to these rules, and one draw needn't show every extreme that they name: `mask_pos`: listed positions may repeat; a position is masked if it is listed at least once.
All inputs are finite; a program needn't handle non-finite values.
Results may differ from the reference program's by a relative error of at most 0.007.
Values may be sent and summed in bfloat16 or wider, within the bound.
A program may use at most 128 MiB of HBM per device.

```python
import jax
import jax.numpy as jnp
from jax import lax

D = 8192
HEAD_DIM = 128
HEADS = 16
SEQS = 2
LEN = 256
NMASK = 64
STEPS = 64
TOKENS = 512


def touch_ends(entries, own_key, least, largest):
    longest = entries.shape.index(max(entries.shape))
    spots = []
    for shift in (0, 1):
        where = [jax.random.randint(jax.random.fold_in(own_key, axis), (), 0, length) for axis, length in enumerate(entries.shape)]
        where[longest] = (where[longest] + shift) % entries.shape[longest]
        spots.append(tuple(where))
    return entries.at[spots[0]].set(least).at[spots[1]].set(largest)


def block_scale(key, shape, cuts, smallest, top_value):
    level = 1.0
    for axis_at, parts in cuts:
        heights = jax.random.uniform(jax.random.fold_in(jax.random.fold_in(key, 6), axis_at), (parts,), jnp.float32, smallest / len(cuts), top_value / len(cuts))
        level = level * jnp.repeat(jnp.exp(heights), shape[axis_at] // parts).reshape((-1,) + (1,) * (len(shape) - 1 - axis_at))
    return level


def normal_values(rng, extent, deviation, most, split=(), kind=jnp.bfloat16):
    entries = jax.random.normal(rng, extent, jnp.float32) * deviation
    if len(split) > 0:
        entries = block_scale(rng, extent, split, -0.22, 0.18) * entries
    return jnp.clip(entries, min=-most, max=most).astype(kind)


def setup_inputs(seed: int = 0, part: int = 0) -> dict:
    seeds = jax.random.split(jax.random.key(seed), 10)
    part_keys = jax.random.split(jax.random.fold_in(seeds[9], part), 10)
    return {
        "tokens_in": normal_values(part_keys[0], (TOKENS, D), 0.5, 4.0, ((0, 16),)),
        "mask_pos": touch_ends(jax.random.randint(part_keys[1], (SEQS, NMASK), 0, LEN), jax.random.fold_in(part_keys[1], 1), 0, LEN - 1).astype(jnp.int32),
        "step_index": jax.random.randint(part_keys[2], (SEQS,), 0, STEPS).astype(jnp.int32),
        "mask_embed": normal_values(seeds[3], (D,), 1.0, 5.0),
        "time_table": normal_values(seeds[4], (STEPS, D), 0.5, 4.0),
        "norm_gain": jnp.clip(1.0 + 0.1 * jax.random.normal(seeds[5], (D,), jnp.float32), 0.5, 1.5),
        "w_qkv": normal_values(seeds[6], (3, D, HEADS * HEAD_DIM), D ** -0.5, 0.0625, ((2, 16),)),
        "qk_gain": jnp.clip(1.0 + 1.0 * jax.random.uniform(seeds[7], (2, HEADS * HEAD_DIM), jnp.float32) ** block_scale(seeds[7], (2, HEADS * HEAD_DIM), ((1, 16),), -0.2, 0.2), 1.0, 2.0),
        "w_out": normal_values(seeds[8], (HEADS * HEAD_DIM, D), HEAD_DIM ** -0.5, 0.5, ((0, 16),)),
    }


def embed_rows(rows_tokens, row_ids, mask_pos, step_index, mask_part, table_part):
    seq_of = row_ids // LEN
    pos_of = row_ids % LEN
    seq_range = jnp.arange(SEQS, dtype=jnp.int32)
    listed = (mask_pos[None, :, :] == pos_of[:, None, None]) & (seq_range[None, :, None] == seq_of[:, None, None])
    masked = jnp.any(listed, axis=(1, 2))
    step_row = lax.optimization_barrier(jnp.sum(jnp.where(seq_range[None, :] == seq_of[:, None], step_index[None, :], 0), axis=1))
    onehot = (step_row[:, None] == jnp.arange(STEPS, dtype=jnp.int32)[None, :]).astype(jnp.bfloat16)
    timed = jnp.dot(onehot, table_part, preferred_element_type=jnp.float32)
    base = jnp.where(masked[:, None], mask_part[None, :].astype(jnp.float32), rows_tokens.astype(jnp.float32))
    return base + timed

def attend(qkv, gains):
    query = qkv[:, 0]
    keys = qkv[:, 1]
    query_n = (query * lax.rsqrt(lax.optimization_barrier(jnp.mean(query * query, axis=-1, keepdims=True)) + 1e-06) * gains[0]).astype(jnp.bfloat16)
    keys_n = (keys * lax.rsqrt(lax.optimization_barrier(jnp.mean(keys * keys, axis=-1, keepdims=True)) + 1e-06) * gains[1]).astype(jnp.bfloat16)
    values = qkv[:, 2].astype(jnp.bfloat16)
    width = qkv.shape[-1]
    query_n = query_n.reshape(SEQS, LEN, width).astype(jnp.float32)
    keys_n = keys_n.reshape(SEQS, LEN, width).astype(jnp.float32)
    values = values.reshape(SEQS, LEN, width).astype(jnp.float32)
    scores = jnp.einsum('sqh,skh->sqk', query_n, keys_n) / jnp.sqrt(jnp.float32(width))
    weights = jnp.exp(scores)
    probs = (weights / lax.optimization_barrier(jnp.sum(weights, axis=-1, keepdims=True))).astype(jnp.bfloat16)
    attn = jnp.einsum('sqk,skh->sqh', probs.astype(jnp.float32), values)
    return attn.reshape(SEQS * LEN, width).astype(jnp.bfloat16)

def reference(tokens_in, mask_pos, step_index, mask_embed, time_table, norm_gain, w_qkv, qk_gain, w_out):
    row_ids = jnp.arange(TOKENS, dtype=jnp.int32)
    embedded = embed_rows(tokens_in, row_ids, mask_pos, step_index, mask_embed, time_table)
    normed = (embedded * lax.rsqrt(lax.optimization_barrier(jnp.mean(embedded * embedded, axis=-1, keepdims=True)) + 1e-05) * norm_gain).astype(jnp.bfloat16)
    weights_by_head = w_qkv.reshape(3, D, HEADS, HEAD_DIM).transpose(2, 0, 1, 3)
    gains_by_head = qk_gain.reshape(2, HEADS, HEAD_DIM).transpose(1, 0, 2)
    normed_wide = normed.astype(jnp.float32)

    def one_head(pair):
        head_weights, head_gains = pair
        qkv = jnp.einsum('td,cdh->tch', normed_wide, head_weights.astype(jnp.float32))
        return attend(qkv, head_gains)
    heads_out = lax.map(one_head, (weights_by_head, gains_by_head))
    attn = heads_out.transpose(1, 0, 2).reshape(TOKENS, HEADS * HEAD_DIM)
    branch = jnp.dot(attn, w_out, preferred_element_type=jnp.float32)
    return (embedded + branch).astype(jnp.bfloat16)
```

```python
import jax
import jax.numpy as jnp
from jax import lax
from jax.sharding import PartitionSpec as P

HEAD_DIM = 128
SEQS = 2
LEN = 256
STEPS = 64


def embed_rows(rows_tokens, row_ids, mask_pos, step_index, mask_part, table_part):
    seq_of = row_ids // LEN
    pos_of = row_ids % LEN
    seq_range = jnp.arange(SEQS, dtype=jnp.int32)
    listed = (mask_pos[None, :, :] == pos_of[:, None, None]) & (
        seq_range[None, :, None] == seq_of[:, None, None]
    )
    masked = jnp.any(listed, axis=(1, 2))
    step_row = jnp.sum(
        jnp.where(seq_range[None, :] == seq_of[:, None], step_index[None, :], 0), axis=1
    )
    onehot = (step_row[:, None] == jnp.arange(STEPS, dtype=jnp.int32)[None, :]).astype(jnp.bfloat16)
    timed = jnp.dot(onehot, table_part, preferred_element_type=jnp.float32)
    base = jnp.where(
        masked[:, None], mask_part[None, :].astype(jnp.float32), rows_tokens.astype(jnp.float32)
    )
    return base + timed


def attend(qkv, gains):
    query = qkv[:, 0]
    keys = qkv[:, 1]
    query_n = (
        query * lax.rsqrt(jnp.mean(query * query, axis=-1, keepdims=True) + 1e-06) * gains[0]
    ).astype(jnp.bfloat16)
    keys_n = (
        keys * lax.rsqrt(jnp.mean(keys * keys, axis=-1, keepdims=True) + 1e-06) * gains[1]
    ).astype(jnp.bfloat16)
    values = qkv[:, 2].astype(jnp.bfloat16)
    width = qkv.shape[-1]
    query_n = query_n.reshape(SEQS, LEN, width)
    keys_n = keys_n.reshape(SEQS, LEN, width)
    values = values.reshape(SEQS, LEN, width)
    scores = jnp.einsum(
        "sqh,skh->sqk", query_n, keys_n, preferred_element_type=jnp.float32
    ) / jnp.sqrt(jnp.float32(width))
    weights = jnp.exp(scores)
    probs = (weights / jnp.sum(weights, axis=-1, keepdims=True)).astype(jnp.bfloat16)
    attn = jnp.einsum("sqk,skh->sqh", probs, values, preferred_element_type=jnp.float32)
    return attn.reshape(SEQS * LEN, width).astype(jnp.bfloat16)


def body(tokens_in, mask_pos, step_index, mask_embed, time_table, norm_gain, w_qkv, qk_gain, w_out):
    my_index = lax.axis_index("tensor")
    col_count = tokens_in.shape[1] // lax.axis_size("tensor")
    w_cols = lax.all_to_all(w_out, "tensor", split_axis=1, concat_axis=0, tiled=True)
    tokens = lax.all_gather(tokens_in, "tensor", axis=0, tiled=True)
    total_rows = tokens.shape[0]
    all_ids = jnp.arange(total_rows, dtype=jnp.int32)
    embedded = embed_rows(tokens, all_ids, mask_pos, step_index, mask_embed, time_table)
    normed = (
        embedded
        * lax.rsqrt(jnp.mean(embedded * embedded, axis=-1, keepdims=True) + 1e-05)
        * norm_gain
    ).astype(jnp.bfloat16)
    qkv = jnp.einsum("td,cdh->tch", normed, w_qkv, preferred_element_type=jnp.float32)
    heads_here = qkv.shape[2] // HEAD_DIM
    qkv_heads = qkv.reshape(total_rows, 3, heads_here, HEAD_DIM)
    gains_heads = qk_gain.reshape(2, heads_here, HEAD_DIM)
    attn = jax.vmap(attend, in_axes=(2, 1), out_axes=1)(qkv_heads, gains_heads)
    attn = attn.reshape(total_rows, heads_here * HEAD_DIM)
    attn_all = lax.all_gather(attn, "tensor", axis=1, tiled=True)
    col_start = my_index * col_count
    embedded_cols = embed_rows(
        lax.dynamic_slice_in_dim(tokens, col_start, col_count, 1),
        all_ids,
        mask_pos,
        step_index,
        lax.dynamic_slice_in_dim(mask_embed, col_start, col_count, 0),
        lax.dynamic_slice_in_dim(time_table, col_start, col_count, 1),
    )
    branch = jnp.dot(attn_all, w_cols, preferred_element_type=jnp.float32)
    return (embedded_cols + branch).astype(jnp.bfloat16)


def solution(mesh):
    return jax.shard_map(
        body,
        mesh=mesh,
        in_specs=(
            P(("groups", "tensor"), None),
            P("groups", None),
            P("groups"),
            P(),
            P(),
            P(),
            P(None, None, "tensor"),
            P(None, "tensor"),
            P("tensor", None),
        ),
        out_specs=P("groups", "tensor"),
        check_vma=False,
    )
```

```python
import jax
import jax.numpy as jnp
from jax import lax
from jax.experimental import pallas as pl
from jax.experimental.pallas import tpu as pltpu
from jax.sharding import PartitionSpec as P

HEAD_DIM = 128
SEQS = 2
LEN = 256
STEPS = 64


def embed_rows(rows_tokens, row_ids, mask_pos, step_index, mask_part, table_part):
    seq_of = row_ids // LEN
    pos_of = row_ids % LEN
    seq_range = jnp.arange(SEQS, dtype=jnp.int32)
    listed = (mask_pos[None, :, :] == pos_of[:, None, None]) & (
        seq_range[None, :, None] == seq_of[:, None, None]
    )
    masked = jnp.any(listed, axis=(1, 2))
    step_row = jnp.sum(
        jnp.where(seq_range[None, :] == seq_of[:, None], step_index[None, :], 0), axis=1
    )
    onehot = (step_row[:, None] == jnp.arange(STEPS, dtype=jnp.int32)[None, :]).astype(jnp.bfloat16)
    timed = jnp.dot(onehot, table_part, preferred_element_type=jnp.float32)
    base = jnp.where(
        masked[:, None], mask_part[None, :].astype(jnp.float32), rows_tokens.astype(jnp.float32)
    )
    return base + timed


def attend(qkv, gains):
    query = qkv[:, 0]
    keys = qkv[:, 1]
    query_n = (
        query * lax.rsqrt(jnp.mean(query * query, axis=-1, keepdims=True) + 1e-06) * gains[0]
    ).astype(jnp.bfloat16)
    keys_n = (
        keys * lax.rsqrt(jnp.mean(keys * keys, axis=-1, keepdims=True) + 1e-06) * gains[1]
    ).astype(jnp.bfloat16)
    values = qkv[:, 2].astype(jnp.bfloat16)
    width = qkv.shape[-1]
    query_n = query_n.reshape(SEQS, LEN, width)
    keys_n = keys_n.reshape(SEQS, LEN, width)
    values = values.reshape(SEQS, LEN, width)
    scores = jnp.einsum(
        "sqh,skh->sqk", query_n, keys_n, preferred_element_type=jnp.float32
    ) / jnp.sqrt(jnp.float32(width))
    weights = jnp.exp(scores)
    probs = (weights / jnp.sum(weights, axis=-1, keepdims=True)).astype(jnp.bfloat16)
    attn = jnp.einsum("sqk,skh->sqh", probs, values, preferred_element_type=jnp.float32)
    return attn.reshape(SEQS * LEN, width).astype(jnp.bfloat16)


def body(tokens_in, mask_pos, step_index, mask_embed, time_table, norm_gain, w_qkv, qk_gain, w_out):
    my_index = lax.axis_index("tensor")
    col_count = tokens_in.shape[1] // lax.axis_size("tensor")
    w_cols = lax.all_to_all(w_out, "tensor", split_axis=1, concat_axis=0, tiled=True)
    tokens = lax.all_gather(tokens_in, "tensor", axis=0, tiled=True)
    total_rows = tokens.shape[0]
    all_ids = jnp.arange(total_rows, dtype=jnp.int32)
    embedded = embed_rows(tokens, all_ids, mask_pos, step_index, mask_embed, time_table)
    normed = (
        embedded
        * lax.rsqrt(jnp.mean(embedded * embedded, axis=-1, keepdims=True) + 1e-05)
        * norm_gain
    ).astype(jnp.bfloat16)
    qkv = jnp.einsum("td,cdh->tch", normed, w_qkv, preferred_element_type=jnp.float32)
    heads_here = qkv.shape[2] // HEAD_DIM
    qkv_heads = qkv.reshape(total_rows, 3, heads_here, HEAD_DIM)
    gains_heads = qk_gain.reshape(2, heads_here, HEAD_DIM)
    attn = jax.vmap(attend, in_axes=(2, 1), out_axes=1)(qkv_heads, gains_heads)
    attn = attn.reshape(total_rows, heads_here * HEAD_DIM)
    attn_all = lax.all_gather(attn, "tensor", axis=1, tiled=True)
    col_start = my_index * col_count
    embedded_cols = embed_rows(
        lax.dynamic_slice_in_dim(tokens, col_start, col_count, 1),
        all_ids,
        mask_pos,
        step_index,
        lax.dynamic_slice_in_dim(mask_embed, col_start, col_count, 0),
        lax.dynamic_slice_in_dim(time_table, col_start, col_count, 1),
    )
    branch = jnp.dot(attn_all, w_cols, preferred_element_type=jnp.float32)
    return (embedded_cols + branch).astype(jnp.bfloat16)


MESH = pl.DeviceIdType.MESH
NZ = 4
NY = 2
CHUNK = 1024


def fused_kernel(
    tok, mpos, step, membed, table, ngain, wqkv, qkg, wout, out,
    xall, wv, wcols, tsc, qkv, att, acc,
    loc, recv, send_z, send_y, send_s, wsend, wrecv, wx, arecv, asend_z, asend_y, asend_s,
):
    n, rows, width = xall.shape
    cols = width // n
    me = lax.axis_index("tensor")
    grp = lax.axis_index("groups")
    core = me % 2
    y = (me // 2) % NY
    z = me // (2 * NY)
    far = z // 2
    zlist = [z, 2 * far + 1 - z % 2, 2 - far, 3 - 3 * far]

    def index(zz, yy, cc):
        return (zz * NY + yy) * 2 + cc

    sibling = index(z, y, 1 - core)
    across = index(z, 1 - y, core)

    own = pltpu.make_async_copy(tok, xall.at[me], loc.at[0])
    own.start()
    wcopies = [
        pltpu.make_async_copy(wqkv.at[c], wv.at[:, pl.ds(c * HEAD_DIM, HEAD_DIM)], loc.at[1 + c]) for c in range(3)
    ]
    for c in wcopies:
        c.start()
    half = wout.shape[0] // 2
    wrows = pl.ds(pl.multiple_of(grp * half, half), half)

    def wblock(d):
        return wout.at[wrows, pl.ds(pl.multiple_of(d * cols, cols), cols)]

    wown = pltpu.make_async_copy(wblock(me), wcols.at[me, grp], loc.at[4])
    wown.start()

    barrier = pltpu.get_barrier_semaphore()

    def greet(i, carry):
        pl.semaphore_signal(barrier, inc=1, device_id={"tensor": (me + i) % n}, device_id_type=MESH)
        return carry

    lax.fori_loop(1, n, greet, 0)
    pl.semaphore_signal(barrier, inc=1, device_id={"groups": 1 - grp}, device_id_type=MESH)
    pl.semaphore_wait(barrier, n)

    def relay(buf, rsem, sz, sy, ss):
        def copy(src, j, sem, to):
            return pltpu.make_async_remote_copy(
                src_ref=src, dst_ref=buf.at[j], send_sem=sem, recv_sem=rsem.at[j],
                device_id={"tensor": to}, device_id_type=MESH,
            )

        def arrived(j):
            copy(buf.at[j], j, sy.at[0], sibling).wait_recv()

        def start_own(src):
            @pl.when(z < NZ - 1)
            def _():
                copy(src, me, sz.at[0], me + 2 * NY).start()

            @pl.when(z > 0)
            def _():
                copy(src, me, sz.at[4], me - 2 * NY).start()

            copy(src, me, sy.at[0], across).start()
            copy(src, me, ss.at[0], sibling).start()

        def onward(k):
            zo = zlist[k]
            nz = jnp.where(zo < z, z + 1, z - 1)
            ok = (nz >= 0) & (nz < NZ)
            return zo, nz, ok

        def z_event(k):
            zo, nz, ok = onward(k)
            j = index(zo, y, core)
            arrived(j)

            @pl.when(ok)
            def _():
                copy(buf.at[j], j, sz.at[k], index(nz, y, core)).start()

            copy(buf.at[j], j, sy.at[k], across).start()
            copy(buf.at[j], j, ss.at[k], sibling).start()

        def y_event(k):
            j = index(zlist[k], 1 - y, core)
            arrived(j)
            copy(buf.at[j], j, ss.at[4 + k], sibling).start()

        def finish(src):
            @pl.when(z < NZ - 1)
            def _():
                copy(src, me, sz.at[0], me + 2 * NY).wait_send()

            @pl.when(z > 0)
            def _():
                copy(src, me, sz.at[4], me - 2 * NY).wait_send()

            for k in range(1, NZ):
                zo, nz, ok = onward(k)
                j = index(zo, y, core)

                @pl.when(ok)
                def _():
                    copy(buf.at[j], j, sz.at[k], index(nz, y, core)).wait_send()

            for k in range(NZ):
                j = index(zlist[k], y, core)
                copy(src if k == 0 else buf.at[j], j, sy.at[k], across).wait_send()
                copy(src if k == 0 else buf.at[j], j, ss.at[k], sibling).wait_send()
                j = index(zlist[k], 1 - y, core)
                copy(buf.at[j], j, ss.at[4 + k], sibling).wait_send()

        return arrived, start_own, z_event, y_event, finish

    x_arrived, x_own, x_z, x_y, x_finish = relay(xall, recv, send_z, send_y, send_s)
    a_arrived, a_own, a_z, a_y, a_finish = relay(att, arecv, asend_z, asend_y, asend_s)

    x_own(tok)

    def wcopy(i):
        d = (me + i) % n
        return pltpu.make_async_remote_copy(
            src_ref=wblock(d), dst_ref=wcols.at[me, grp], send_sem=wsend.at[i], recv_sem=wrecv.at[me],
            device_id={"tensor": d}, device_id_type=MESH,
        )

    def wstart(i, carry):
        wcopy(i).start()
        return carry

    lax.fori_loop(1, n, wstart, 0)

    lanes = lax.broadcasted_iota(jnp.int32, (SEQS, STEPS), 1)
    onehot = jnp.where(lanes == step[...], 1.0, 0.0).astype(jnp.bfloat16)

    def timed(i, carry):
        at = pl.ds(pl.multiple_of(i * CHUNK, CHUNK), CHUNK)
        both = jnp.dot(onehot, table[:, at], preferred_element_type=jnp.float32)
        for s in range(SEQS):
            tsc[s, :, at] = both[s : s + 1]
        return carry

    lax.fori_loop(0, width // CHUNK, timed, 0)

    tall = 2 * rows
    per_seq = LEN // tall

    def masked_rows(chip):
        pos = (chip % per_seq) * tall + lax.broadcasted_iota(jnp.int32, (tall, mpos.shape[-1]), 0)
        hit = jnp.where(pos == mpos[chip // per_seq], 1.0, 0.0)
        return jnp.max(hit, axis=1, keepdims=True)

    def embedded(chip, hit, at, size):
        raw = xall[pl.ds(2 * chip, 2), :, at].astype(jnp.float32).reshape(tall, size)
        base = jnp.where(hit > 0.5, membed[:, at].astype(jnp.float32), raw)
        return base + tsc[chip // per_seq, :, at]

    def project(chip):
        hit = masked_rows(chip)

        def squares(i, total):
            at = pl.ds(pl.multiple_of(i * CHUNK, CHUNK), CHUNK)
            e = embedded(chip, hit, at, CHUNK)
            e = e * e
            for p in range(CHUNK // 128):
                total = total + e[:, p * 128 : (p + 1) * 128]
            return total

        total = lax.fori_loop(0, width // CHUNK, squares, jnp.zeros((tall, 128), jnp.float32))
        scale = lax.rsqrt(jnp.sum(total, axis=1, keepdims=True) / width + 1e-05)

        def multiply(i, total):
            at = pl.ds(pl.multiple_of(i * CHUNK, CHUNK), CHUNK)
            normed = (embedded(chip, hit, at, CHUNK) * scale * ngain[:, at]).astype(jnp.bfloat16)
            return total + jnp.dot(normed, wv[at, :], preferred_element_type=jnp.float32)

        qkv[chip] = lax.fori_loop(
            0, width // CHUNK, multiply, jnp.zeros((tall, 3 * HEAD_DIM), jnp.float32)
        )

    def chip_of(k, yy):
        return zlist[k] * NY + yy

    def attend_one(s):
        block = qkv[pl.ds(s * per_seq, per_seq)].reshape(LEN, 3 * HEAD_DIM)
        q = block[:, :HEAD_DIM]
        k = block[:, HEAD_DIM : 2 * HEAD_DIM]
        v = block[:, 2 * HEAD_DIM :].astype(jnp.bfloat16)
        qn = (q * lax.rsqrt(jnp.mean(q * q, axis=1, keepdims=True) + 1e-06) * qkg[0:1, :]).astype(jnp.bfloat16)
        kn = (k * lax.rsqrt(jnp.mean(k * k, axis=1, keepdims=True) + 1e-06) * qkg[1:2, :]).astype(jnp.bfloat16)
        scores = lax.dot_general(qn, kn, (((1,), (1,)), ((), ())), preferred_element_type=jnp.float32)
        weights = jnp.exp(scores * (HEAD_DIM**-0.5))
        probs = (weights / jnp.sum(weights, axis=1, keepdims=True)).astype(jnp.bfloat16)
        att[me, pl.ds(pl.multiple_of(s * LEN, LEN), LEN), :] = jnp.dot(
            probs, v, preferred_element_type=jnp.float32
        ).astype(jnp.bfloat16)

    inner = (z > 0) & (z < NZ - 1)

    own.wait()
    for c in wcopies:
        c.wait()
    x_arrived(sibling)
    project(chip_of(0, y))
    x_z(1)

    @pl.when(inner)
    def _():
        x_z(2)

    x_arrived(index(zlist[1], y, 1 - core))
    project(chip_of(1, y))
    x_y(0)

    @pl.when(inner)
    def _():
        x_z(3)

    x_arrived(index(zlist[0], 1 - y, 1 - core))
    project(chip_of(0, 1 - y))

    @pl.when(jnp.logical_not(inner))
    def _():
        x_z(2)

    x_y(1)
    x_arrived(index(zlist[1], 1 - y, 1 - core))
    project(chip_of(1, 1 - y))
    x_arrived(index(zlist[2], y, 1 - core))
    project(chip_of(2, y))

    @pl.when(jnp.logical_not(inner))
    def _():
        x_z(3)

    attend_one(far)
    x_y(2)
    x_arrived(index(zlist[3], y, 1 - core))
    project(chip_of(3, y))
    x_arrived(index(zlist[2], 1 - y, 1 - core))
    project(chip_of(2, 1 - y))
    x_y(3)
    x_arrived(index(zlist[3], 1 - y, 1 - core))
    project(chip_of(3, 1 - y))
    attend_one(1 - far)
    a_own(att.at[me])

    wown.wait()

    def wwait(i, carry):
        j = (me + i) % n
        pltpu.make_async_remote_copy(
            src_ref=wcols.at[j, grp], dst_ref=wcols.at[j, grp], send_sem=wsend.at[i], recv_sem=wrecv.at[j],
            device_id={"tensor": j}, device_id_type=MESH,
        ).wait_recv()
        return carry

    lax.fori_loop(1, n, wwait, 0)
    wshare = pltpu.make_async_remote_copy(
        src_ref=wcols.at[:, grp], dst_ref=wcols.at[:, grp], send_sem=wx.at[0], recv_sem=wx.at[1],
        device_id={"groups": 1 - grp}, device_id_type=MESH,
    )
    wshare.start()
    a_z(1)

    @pl.when(inner)
    def _():
        a_z(2)

    mine = pl.ds(pl.multiple_of(me * cols, cols), cols)

    def residual(chip, carry):
        acc[pl.ds(pl.multiple_of(chip * tall, tall), tall), :] = embedded(chip, masked_rows(chip), mine, cols)
        return carry

    lax.fori_loop(0, SEQS * per_seq, residual, 0)

    @pl.when(jnp.logical_not(inner))
    def _():
        a_z(2)

    a_z(3)
    pltpu.make_async_remote_copy(
        src_ref=wcols.at[:, 1 - grp], dst_ref=wcols.at[:, 1 - grp], send_sem=wx.at[0], recv_sem=wx.at[1],
        device_id={"groups": 1 - grp}, device_id_type=MESH,
    ).wait_recv()

    def head_pair(chip):
        left = jnp.concatenate([att[2 * chip], att[2 * chip + 1]], axis=1)
        right = wcols[pl.ds(2 * chip, 2)].reshape(2 * HEAD_DIM, cols)
        acc[...] += jnp.dot(left, right, preferred_element_type=jnp.float32)

    a_arrived(sibling)
    head_pair(chip_of(0, y))
    for k in range(1, NZ):
        a_y(k - 1)
        a_arrived(index(zlist[k], y, 1 - core))
        head_pair(chip_of(k, y))
    a_y(3)
    for k in range(NZ):
        a_arrived(index(zlist[k], 1 - y, 1 - core))
        head_pair(chip_of(k, 1 - y))
    out[...] = acc[...].astype(jnp.bfloat16)

    x_finish(tok)
    a_finish(att.at[me])

    def wdone(i, carry):
        wcopy(i).wait_send()
        return carry

    lax.fori_loop(1, n, wdone, 0)
    wshare.wait_send()


def fused(tokens_in, mask_pos, step_index, mask_embed, time_table, norm_gain, w_qkv, qk_gain, w_out):
    n = lax.axis_size("tensor")
    rows, width = tokens_in.shape
    total = n * rows
    cols = width // n
    vmem = pl.BlockSpec(memory_space=pltpu.VMEM)
    hbm = pl.BlockSpec(memory_space=pl.ANY)
    dma = pltpu.SemaphoreType.DMA
    return pl.pallas_call(
        fused_kernel,
        out_shape=jax.ShapeDtypeStruct((total, cols), jnp.bfloat16),
        in_specs=[hbm, vmem, vmem, vmem, vmem, vmem, hbm, vmem, hbm],
        out_specs=vmem,
        scratch_shapes=[
            pltpu.VMEM((n, rows, width), jnp.bfloat16),
            pltpu.VMEM((width, 3 * HEAD_DIM), jnp.bfloat16),
            pltpu.VMEM((n, 2, HEAD_DIM // 2, cols), jnp.bfloat16),
            pltpu.VMEM((SEQS, 1, width), jnp.float32),
            pltpu.VMEM((n // 2, 2 * rows, 3 * HEAD_DIM), jnp.float32),
            pltpu.VMEM((n, total, HEAD_DIM), jnp.bfloat16),
            pltpu.VMEM((total, cols), jnp.float32),
            dma((5,)), dma((n,)), dma((5,)), dma((4,)), dma((8,)), dma((n,)), dma((n,)), dma((2,)),
            dma((n,)), dma((5,)), dma((4,)), dma((8,)),
        ],
        compiler_params=pltpu.CompilerParams(
            collective_id=0, has_side_effects=True, vmem_limit_bytes=48 * 1024 * 1024
        ),
        cost_estimate=pl.CostEstimate(flops=2 * total * width * 3 * HEAD_DIM, bytes_accessed=10 * 1024 * 1024, transcendentals=0),
    )(
        tokens_in, mask_pos.reshape(SEQS, 1, -1), step_index.reshape(SEQS, 1), mask_embed.reshape(1, width),
        time_table, norm_gain.reshape(1, width), w_qkv, qk_gain, w_out,
    )


def solution(mesh):
    def run(tokens_in, mask_pos, step_index, mask_embed, time_table, norm_gain, w_qkv, qk_gain, w_out):
        fits = (
            mesh.shape["tensor"] == 2 * NY * NZ
            and mesh.shape["groups"] == 2
            and w_qkv.shape[2] == HEAD_DIM
            and tokens_in.shape[0] % 16 == 0
            and tokens_in.shape[0] * mesh.shape["tensor"] == SEQS * LEN
        )
        return (fused if fits else body)(
            tokens_in, mask_pos, step_index, mask_embed, time_table, norm_gain, w_qkv, qk_gain, w_out
        )

    return jax.shard_map(
        run,
        mesh=mesh,
        in_specs=(
            P(("groups", "tensor"), None),
            P("groups", None),
            P("groups"),
            P(),
            P(),
            P(),
            P(None, None, "tensor"),
            P(None, "tensor"),
            P("tensor", None),
        ),
        out_specs=P("groups", "tensor"),
        check_vma=False,
    )
```

```python
import jax
import jax.numpy as jnp
from jax import lax
from jax.experimental import pallas as pl
from jax.experimental.pallas import tpu as pltpu
from jax.sharding import PartitionSpec as P

HEAD_DIM = 128
SEQS = 2
LEN = 256
STEPS = 64


def embed_rows(rows_tokens, row_ids, mask_pos, step_index, mask_part, table_part):
    seq_of = row_ids // LEN
    pos_of = row_ids % LEN
    seq_range = jnp.arange(SEQS, dtype=jnp.int32)
    listed = (mask_pos[None, :, :] == pos_of[:, None, None]) & (
        seq_range[None, :, None] == seq_of[:, None, None]
    )
    masked = jnp.any(listed, axis=(1, 2))
    step_row = jnp.sum(
        jnp.where(seq_range[None, :] == seq_of[:, None], step_index[None, :], 0), axis=1
    )
    onehot = (step_row[:, None] == jnp.arange(STEPS, dtype=jnp.int32)[None, :]).astype(jnp.bfloat16)
    timed = jnp.dot(onehot, table_part, preferred_element_type=jnp.float32)
    base = jnp.where(
        masked[:, None], mask_part[None, :].astype(jnp.float32), rows_tokens.astype(jnp.float32)
    )
    return base + timed


def attend(qkv, gains):
    query = qkv[:, 0]
    keys = qkv[:, 1]
    query_n = (
        query * lax.rsqrt(jnp.mean(query * query, axis=-1, keepdims=True) + 1e-06) * gains[0]
    ).astype(jnp.bfloat16)
    keys_n = (
        keys * lax.rsqrt(jnp.mean(keys * keys, axis=-1, keepdims=True) + 1e-06) * gains[1]
    ).astype(jnp.bfloat16)
    values = qkv[:, 2].astype(jnp.bfloat16)
    width = qkv.shape[-1]
    query_n = query_n.reshape(SEQS, LEN, width)
    keys_n = keys_n.reshape(SEQS, LEN, width)
    values = values.reshape(SEQS, LEN, width)
    scores = jnp.einsum(
        "sqh,skh->sqk", query_n, keys_n, preferred_element_type=jnp.float32
    ) / jnp.sqrt(jnp.float32(width))
    weights = jnp.exp(scores)
    probs = (weights / jnp.sum(weights, axis=-1, keepdims=True)).astype(jnp.bfloat16)
    attn = jnp.einsum("sqk,skh->sqh", probs, values, preferred_element_type=jnp.float32)
    return attn.reshape(SEQS * LEN, width).astype(jnp.bfloat16)


def body(tokens_in, mask_pos, step_index, mask_embed, time_table, norm_gain, w_qkv, qk_gain, w_out):
    my_index = lax.axis_index("tensor")
    col_count = tokens_in.shape[1] // lax.axis_size("tensor")
    w_cols = lax.all_to_all(w_out, "tensor", split_axis=1, concat_axis=0, tiled=True)
    tokens = lax.all_gather(tokens_in, "tensor", axis=0, tiled=True)
    total_rows = tokens.shape[0]
    all_ids = jnp.arange(total_rows, dtype=jnp.int32)
    embedded = embed_rows(tokens, all_ids, mask_pos, step_index, mask_embed, time_table)
    normed = (
        embedded
        * lax.rsqrt(jnp.mean(embedded * embedded, axis=-1, keepdims=True) + 1e-05)
        * norm_gain
    ).astype(jnp.bfloat16)
    qkv = jnp.einsum("td,cdh->tch", normed, w_qkv, preferred_element_type=jnp.float32)
    heads_here = qkv.shape[2] // HEAD_DIM
    qkv_heads = qkv.reshape(total_rows, 3, heads_here, HEAD_DIM)
    gains_heads = qk_gain.reshape(2, heads_here, HEAD_DIM)
    attn = jax.vmap(attend, in_axes=(2, 1), out_axes=1)(qkv_heads, gains_heads)
    attn = attn.reshape(total_rows, heads_here * HEAD_DIM)
    attn_all = lax.all_gather(attn, "tensor", axis=1, tiled=True)
    col_start = my_index * col_count
    embedded_cols = embed_rows(
        lax.dynamic_slice_in_dim(tokens, col_start, col_count, 1),
        all_ids,
        mask_pos,
        step_index,
        lax.dynamic_slice_in_dim(mask_embed, col_start, col_count, 0),
        lax.dynamic_slice_in_dim(time_table, col_start, col_count, 1),
    )
    branch = jnp.dot(attn_all, w_cols, preferred_element_type=jnp.float32)
    return (embedded_cols + branch).astype(jnp.bfloat16)


MESH = pl.DeviceIdType.MESH
NZ = 4
NY = 2
CHUNK = 1024


def fused_kernel(
    tok, mpos_h, step, membed_h, table_h, ngain_h, wqkv, qkg_h, wout, out,
    mpos, membed, table, ngain, qkg, xall, wv, wcols, tsc, qkv, att, acc,
    loc, recv, send_z, send_y, send_s, wsend, wrecv, wx_s, wx_r, arecv, asend_z, asend_y, asend_s, brecv, bsend_z, bsend_y, bsend_s,
):
    n, rows, width = xall.shape
    cols = width // n
    me = lax.axis_index("tensor")
    grp = lax.axis_index("groups")
    core = me % 2
    y = (me // 2) % NY
    z = me // (2 * NY)
    far = z // 2
    zlist = [z, 2 * far + 1 - z % 2, 2 - far, 3 - 3 * far]

    def index(zz, yy, cc):
        return (zz * NY + yy) * 2 + cc

    sibling = index(z, y, 1 - core)
    across = index(z, 1 - y, core)

    own = pltpu.make_async_copy(tok, xall.at[me], loc.at[0])
    own.start()
    wcopies = [
        pltpu.make_async_copy(wqkv.at[c], wv.at[:, pl.ds(c * HEAD_DIM, HEAD_DIM)], loc.at[1 + c]) for c in range(3)
    ]
    for c in wcopies:
        c.start()
    half = wout.shape[0] // 2
    wrows = pl.ds(pl.multiple_of(grp * half, half), half)

    def wblock(d):
        return wout.at[wrows, pl.ds(pl.multiple_of(d * cols, cols), cols)]

    wown = pltpu.make_async_copy(wblock(me), wcols.at[me, grp], loc.at[4])
    wown.start()

    small = [
        pltpu.make_async_copy(src, dst, loc.at[5 + i])
        for i, (src, dst) in enumerate(
            [(mpos_h, mpos), (membed_h, membed), (table_h, table), (ngain_h, ngain), (qkg_h, qkg)]
        )
    ]
    for c in small:
        c.start()

    barrier = pltpu.get_barrier_semaphore()

    def greet(i, carry):
        pl.semaphore_signal(barrier, inc=1, device_id={"tensor": (me + i) % n}, device_id_type=MESH)
        return carry

    lax.fori_loop(1, n, greet, 0)
    pl.semaphore_signal(barrier, inc=1, device_id={"groups": 1 - grp}, device_id_type=MESH)
    pl.semaphore_wait(barrier, n)

    def relay(slot, rsem, sz, sy, ss):
        def copy(src, j, sem, to):
            return pltpu.make_async_remote_copy(
                src_ref=src, dst_ref=slot(j), send_sem=sem, recv_sem=rsem.at[j],
                device_id={"tensor": to}, device_id_type=MESH,
            )

        def arrived(j):
            copy(slot(j), j, sy.at[0], sibling).wait_recv()

        def start_own(src):
            @pl.when(z < NZ - 1)
            def _():
                copy(src, me, sz.at[0], me + 2 * NY).start()

            @pl.when(z > 0)
            def _():
                copy(src, me, sz.at[4], me - 2 * NY).start()

            copy(src, me, sy.at[0], across).start()
            copy(src, me, ss.at[0], sibling).start()

        def onward(k):
            zo = zlist[k]
            nz = jnp.where(zo < z, z + 1, z - 1)
            ok = (nz >= 0) & (nz < NZ)
            return zo, nz, ok

        def z_event(k):
            zo, nz, ok = onward(k)
            j = index(zo, y, core)
            arrived(j)

            @pl.when(ok)
            def _():
                copy(slot(j), j, sz.at[k], index(nz, y, core)).start()

            copy(slot(j), j, sy.at[k], across).start()
            copy(slot(j), j, ss.at[k], sibling).start()

        def y_event(k):
            j = index(zlist[k], 1 - y, core)
            arrived(j)
            copy(slot(j), j, ss.at[4 + k], sibling).start()

        def finish(src):
            @pl.when(z < NZ - 1)
            def _():
                copy(src, me, sz.at[0], me + 2 * NY).wait_send()

            @pl.when(z > 0)
            def _():
                copy(src, me, sz.at[4], me - 2 * NY).wait_send()

            for k in range(1, NZ):
                zo, nz, ok = onward(k)
                j = index(zo, y, core)

                @pl.when(ok)
                def _():
                    copy(slot(j), j, sz.at[k], index(nz, y, core)).wait_send()

            for k in range(NZ):
                j = index(zlist[k], y, core)
                copy(src if k == 0 else slot(j), j, sy.at[k], across).wait_send()
                copy(src if k == 0 else slot(j), j, ss.at[k], sibling).wait_send()
                j = index(zlist[k], 1 - y, core)
                copy(slot(j), j, ss.at[4 + k], sibling).wait_send()

        return arrived, start_own, z_event, y_event, finish

    def part(first):
        def slot(j):
            s = (j // (2 * NY)) // 2
            s = s if first else 1 - s
            return att.at[j, pl.ds(pl.multiple_of(s * LEN, LEN), LEN)]

        return slot

    x_arrived, x_own, x_z, x_y, x_finish = relay(lambda j: xall.at[j], recv, send_z, send_y, send_s)
    a_arrived, a_own, a_z, a_y, a_finish = relay(part(True), arecv, asend_z, asend_y, asend_s)
    b_arrived, b_own, b_z, b_y, b_finish = relay(part(False), brecv, bsend_z, bsend_y, bsend_s)

    x_own(tok)

    def wcopy(i):
        d = (me + i) % n
        return pltpu.make_async_remote_copy(
            src_ref=wblock(d), dst_ref=wcols.at[me, grp], send_sem=wsend.at[i], recv_sem=wrecv.at[me],
            device_id={"tensor": d}, device_id_type=MESH,
        )

    def wstart(i, carry):
        wcopy(i).start()
        return carry

    for c in small:
        c.wait()

    lanes = lax.broadcasted_iota(jnp.int32, (SEQS, STEPS), 1)
    which = lax.broadcasted_iota(jnp.int32, (SEQS, STEPS), 0)
    chosen = jnp.where(which == 0, step[0], step[1])
    onehot = jnp.where(lanes == chosen, 1.0, 0.0).astype(jnp.bfloat16)

    def timed(i, carry):
        at = pl.ds(pl.multiple_of(i * CHUNK, CHUNK), CHUNK)
        both = jnp.dot(onehot, table[:, at], preferred_element_type=jnp.float32)
        for s in range(SEQS):
            tsc[s, :, at] = both[s : s + 1]
        return carry

    lax.fori_loop(0, width // CHUNK, timed, 0)

    tall = 2 * rows
    per_seq = LEN // tall

    def masked_rows(chip):
        pos = (chip % per_seq) * tall + lax.broadcasted_iota(jnp.int32, (tall, mpos.shape[-1]), 0)
        hit = jnp.where(pos == mpos[chip // per_seq], 1.0, 0.0)
        return jnp.max(hit, axis=1, keepdims=True)

    def embedded(chip, hit, at, size):
        raw = xall[pl.ds(2 * chip, 2), :, at].astype(jnp.float32).reshape(tall, size)
        base = jnp.where(hit > 0.5, membed[:, at].astype(jnp.float32), raw)
        return base + tsc[chip // per_seq, :, at]

    def project(chip):
        hit = masked_rows(chip)

        def squares(i, total):
            at = pl.ds(pl.multiple_of(i * CHUNK, CHUNK), CHUNK)
            e = embedded(chip, hit, at, CHUNK)
            e = e * e
            for p in range(CHUNK // 128):
                total = total + e[:, p * 128 : (p + 1) * 128]
            return total

        total = lax.fori_loop(0, width // CHUNK, squares, jnp.zeros((tall, 128), jnp.float32))
        scale = lax.rsqrt(jnp.sum(total, axis=1, keepdims=True) / width + 1e-05)

        def multiply(i, total):
            at = pl.ds(pl.multiple_of(i * CHUNK, CHUNK), CHUNK)
            normed = (embedded(chip, hit, at, CHUNK) * scale * ngain[:, at]).astype(jnp.bfloat16)
            return total + jnp.dot(normed, wv[at, :], preferred_element_type=jnp.float32)

        qkv[chip] = lax.fori_loop(
            0, width // CHUNK, multiply, jnp.zeros((tall, 3 * HEAD_DIM), jnp.float32)
        )

    def chip_of(k, yy):
        return zlist[k] * NY + yy

    def attend_one(s):
        block = qkv[pl.ds(s * per_seq, per_seq)].reshape(LEN, 3 * HEAD_DIM)
        q = block[:, :HEAD_DIM]
        k = block[:, HEAD_DIM : 2 * HEAD_DIM]
        v = block[:, 2 * HEAD_DIM :].astype(jnp.bfloat16)
        qn = (q * lax.rsqrt(jnp.mean(q * q, axis=1, keepdims=True) + 1e-06) * qkg[0:1, :]).astype(jnp.bfloat16)
        kn = (k * lax.rsqrt(jnp.mean(k * k, axis=1, keepdims=True) + 1e-06) * qkg[1:2, :]).astype(jnp.bfloat16)
        scores = lax.dot_general(qn, kn, (((1,), (1,)), ((), ())), preferred_element_type=jnp.float32)
        weights = jnp.exp(scores * (HEAD_DIM**-0.5))
        probs = (weights / jnp.sum(weights, axis=1, keepdims=True)).astype(jnp.bfloat16)
        att[me, pl.ds(pl.multiple_of(s * LEN, LEN), LEN), :] = jnp.dot(
            probs, v, preferred_element_type=jnp.float32
        ).astype(jnp.bfloat16)

    inner = (z > 0) & (z < NZ - 1)

    own.wait()
    for c in wcopies:
        c.wait()
    x_arrived(sibling)
    project(chip_of(0, y))
    x_z(1)

    @pl.when(inner)
    def _():
        x_z(2)

    x_arrived(index(zlist[1], y, 1 - core))
    project(chip_of(1, y))
    x_y(0)

    @pl.when(inner)
    def _():
        x_z(3)

    x_arrived(index(zlist[0], 1 - y, 1 - core))
    project(chip_of(0, 1 - y))

    @pl.when(jnp.logical_not(inner))
    def _():
        x_z(2)

    lax.fori_loop(1, n, wstart, 0)
    x_y(1)
    x_arrived(index(zlist[1], 1 - y, 1 - core))
    project(chip_of(1, 1 - y))
    attend_one(far)
    a_own(part(True)(me))
    x_arrived(index(zlist[2], y, 1 - core))
    project(chip_of(2, y))

    @pl.when(jnp.logical_not(inner))
    def _():
        x_z(3)

    x_y(2)
    x_arrived(index(zlist[3], y, 1 - core))
    project(chip_of(3, y))
    a_z(1)

    @pl.when(inner)
    def _():
        a_z(2)

    wown.wait()

    def wshare(zz, own_half):
        blocks = pl.ds(2 * NY * zz, 2 * NY)
        g = grp if own_half else 1 - grp
        return pltpu.make_async_remote_copy(
            src_ref=wcols.at[blocks, g], dst_ref=wcols.at[blocks, g], send_sem=wx_s.at[zz], recv_sem=wx_r.at[zz],
            device_id={"groups": 1 - grp}, device_id_type=MESH,
        )

    def share(zz):
        def wwait(i, carry):
            j = 2 * NY * zz + i

            @pl.when(j != me)
            def _():
                pltpu.make_async_remote_copy(
                    src_ref=wcols.at[j, grp], dst_ref=wcols.at[j, grp], send_sem=wsend.at[i], recv_sem=wrecv.at[j],
                    device_id={"tensor": sibling}, device_id_type=MESH,
                ).wait_recv()

            return carry

        lax.fori_loop(0, 2 * NY, wwait, 0)
        wshare(zz, True).start()

    share(zlist[0])
    x_arrived(index(zlist[2], 1 - y, 1 - core))
    project(chip_of(2, 1 - y))

    @pl.when(jnp.logical_not(inner))
    def _():
        a_z(2)

    a_z(3)
    share(zlist[1])
    x_y(3)
    x_arrived(index(zlist[3], 1 - y, 1 - core))
    project(chip_of(3, 1 - y))
    attend_one(1 - far)
    b_own(part(False)(me))
    for k in range(NZ):
        a_y(k)
    share(zlist[2])
    b_z(1)

    @pl.when(inner)
    def _():
        b_z(2)

    share(zlist[3])
    b_y(0)
    mine = pl.ds(pl.multiple_of(me * cols, cols), cols)

    def residual(chip, carry):
        acc[pl.ds(pl.multiple_of(chip * tall, tall), tall), :] = embedded(chip, masked_rows(chip), mine, cols)
        return carry

    lax.fori_loop(0, SEQS * per_seq, residual, 0)

    @pl.when(jnp.logical_not(inner))
    def _():
        b_z(2)

    b_z(3)
    b_y(1)

    def head_pair(chip):
        left = jnp.concatenate([att[2 * chip], att[2 * chip + 1]], axis=1)
        right = wcols[pl.ds(2 * chip, 2)].reshape(2 * HEAD_DIM, cols)
        acc[...] += jnp.dot(left, right, preferred_element_type=jnp.float32)

    def ready(k, yy):
        a_arrived(index(zlist[k], yy, 1 - core))
        b_arrived(index(zlist[k], yy, 1 - core))
        head_pair(chip_of(k, yy))

    wshare(zlist[0], False).wait_recv()
    ready(0, y)
    ready(0, 1 - y)
    wshare(zlist[1], False).wait_recv()
    ready(1, y)
    b_y(2)
    ready(1, 1 - y)
    wshare(zlist[2], False).wait_recv()
    ready(2, y)
    b_y(3)
    wshare(zlist[3], False).wait_recv()
    ready(3, y)
    ready(2, 1 - y)
    ready(3, 1 - y)
    out[...] = acc[...].astype(jnp.bfloat16)

    x_finish(tok)
    a_finish(part(True)(me))
    b_finish(part(False)(me))

    def wdone(i, carry):
        wcopy(i).wait_send()
        return carry

    lax.fori_loop(1, n, wdone, 0)
    for zz in range(NZ):
        wshare(zz, True).wait_send()


def fused(tokens_in, mask_pos, step_index, mask_embed, time_table, norm_gain, w_qkv, qk_gain, w_out):
    n = lax.axis_size("tensor")
    rows, width = tokens_in.shape
    total = n * rows
    cols = width // n
    vmem = pl.BlockSpec(memory_space=pltpu.VMEM)
    hbm = pl.BlockSpec(memory_space=pl.ANY)
    dma = pltpu.SemaphoreType.DMA
    return pl.pallas_call(
        fused_kernel,
        out_shape=jax.ShapeDtypeStruct((total, cols), jnp.bfloat16),
        in_specs=[hbm, hbm, pl.BlockSpec(memory_space=pltpu.SMEM)] + [hbm] * 6,
        out_specs=vmem,
        scratch_shapes=[
            pltpu.VMEM((SEQS, 1, mask_pos.shape[1]), jnp.int32),
            pltpu.VMEM((1, width), jnp.bfloat16),
            pltpu.VMEM(time_table.shape, jnp.bfloat16),
            pltpu.VMEM((1, width), jnp.float32),
            pltpu.VMEM(qk_gain.shape, jnp.float32),
            pltpu.VMEM((n, rows, width), jnp.bfloat16),
            pltpu.VMEM((width, 3 * HEAD_DIM), jnp.bfloat16),
            pltpu.VMEM((n, 2, HEAD_DIM // 2, cols), jnp.bfloat16),
            pltpu.VMEM((SEQS, 1, width), jnp.float32),
            pltpu.VMEM((n // 2, 2 * rows, 3 * HEAD_DIM), jnp.float32),
            pltpu.VMEM((n, total, HEAD_DIM), jnp.bfloat16),
            pltpu.VMEM((total, cols), jnp.float32),
            dma((10,)), dma((n,)), dma((5,)), dma((4,)), dma((8,)), dma((n,)), dma((n,)), dma((4,)), dma((4,)),
            dma((n,)), dma((5,)), dma((4,)), dma((8,)), dma((n,)), dma((5,)), dma((4,)), dma((8,)),
        ],
        compiler_params=pltpu.CompilerParams(
            collective_id=0, has_side_effects=True, vmem_limit_bytes=48 * 1024 * 1024
        ),
        cost_estimate=pl.CostEstimate(flops=2 * total * width * 3 * HEAD_DIM, bytes_accessed=10 * 1024 * 1024, transcendentals=0),
    )(
        tokens_in, mask_pos.reshape(SEQS, 1, -1), step_index, mask_embed.reshape(1, width),
        time_table, norm_gain.reshape(1, width), w_qkv, qk_gain, w_out,
    )


def solution(mesh):
    def run(tokens_in, mask_pos, step_index, mask_embed, time_table, norm_gain, w_qkv, qk_gain, w_out):
        fits = (
            mesh.shape["tensor"] == 2 * NY * NZ
            and mesh.shape["groups"] == 2
            and w_qkv.shape[2] == HEAD_DIM
            and tokens_in.shape[0] % 16 == 0
            and tokens_in.shape[0] * mesh.shape["tensor"] == SEQS * LEN
        )
        return (fused if fits else body)(
            tokens_in, mask_pos, step_index, mask_embed, time_table, norm_gain, w_qkv, qk_gain, w_out
        )

    return jax.shard_map(
        run,
        mesh=mesh,
        in_specs=(
            P(("groups", "tensor"), None),
            P("groups", None),
            P("groups"),
            P(),
            P(),
            P(),
            P(None, None, "tensor"),
            P(None, "tensor"),
            P("tensor", None),
        ),
        out_specs=P("groups", "tensor"),
        check_vma=False,
    )
```
